512 devices in a mesh: dp: 64 (over x, z, core), tensor: 8 (over y).
Axes of the slice: x: 4, y: 8, z: 8, core: 2. Of those that a mesh axis runs over, the one named last changes fastest.
Arguments:
- activations: bfloat16 [64, 1024, 5120], P('dp', 'tensor'), may hold values from -6 to 6
- out_grads: bfloat16 [64, 1024, 1024], P('dp', None, 'tensor'), may hold values from -0.1875 to 0.1875
- residual: bfloat16 [64, 5120, 1024], P('dp', None, 'tensor'), may hold values from -6 to 6
- q_start: float32 [1024, 32], P('tensor'), may hold values from -6 to 6
Outputs:
- p_factor: float32 [5120, 32], P('tensor')
- q_factor: float32 [1024, 32], P('tensor')
- residual_out: bfloat16 [64, 5120, 1024], P('dp', None, 'tensor')
The draws below stay inside these ranges and needn't reach their ends.
All inputs are finite; a program needn't handle non-finite values.
Results may differ from the reference program's by a relative error of at most 0.0005.
Values may be sent and summed in bfloat16 or wider, within the bound.
No kernel may reach another device: no remote copies, remote signals or barrier semaphores. Data moves between devices by JAX's collectives and lax.ppermute only.
A program may use at most 64 MiB of HBM per device.

```python
import jax
import jax.numpy as jnp
from jax import lax

D = 5120
COLS = 1024
R = 32
TOKENS = 1024
REPLICAS = 64


def shard_levels(rng, extent, cuts, low, largest):
    def one(axis_at, shards_of):
        heights = jax.random.uniform(jax.random.fold_in(jax.random.fold_in(rng, 6), axis_at), (shards_of,), jnp.float32, low / len(cuts), largest / len(cuts))
        return jnp.repeat(jnp.exp(heights), extent[axis_at] // shards_of).reshape((-1,) + (1,) * (len(extent) - axis_at - 1))

    loudness = one(*cuts[0])
    for cut in cuts[1:]:
        loudness = loudness * one(*cut)
    return loudness


def centred(rng, dims, deviation, bound, split=(), held_as=jnp.bfloat16):
    drawn = deviation * jax.random.normal(rng, dims, jnp.float32)
    if split:
        drawn = drawn * shard_levels(rng, dims, split, -0.22, 0.18)
    return jnp.clip(drawn, -bound, bound).astype(held_as)


def setup_inputs(seed: int = 0) -> dict:
    key_of = jax.random.split(jax.random.key(seed), 5)
    activations = centred(key_of[0], (REPLICAS, TOKENS, D), 1.0, 6.0, ((0, 64), (1, 8)))
    out_grads = centred(key_of[1], (REPLICAS, TOKENS, COLS), TOKENS ** -0.5, 0.1875, ((0, 64), (2, 8)))
    residual = centred(key_of[2], (REPLICAS, D, COLS), 1.0, 6.0, ((0, 64), (2, 8)))
    q_start = centred(key_of[3], (COLS, R), 1.0, 6.0, ((0, 8),), jnp.float32)
    return {"activations": activations, "out_grads": out_grads, "residual": residual, "q_start": q_start}


def reference(activations, out_grads, residual, q_start):
    replicas = activations.shape[0]
    width = activations.shape[2]
    highest = lax.Precision.HIGHEST

    def merge_one(index):
        gradient = jnp.dot(activations[index].T.astype(jnp.float32), out_grads[index].astype(jnp.float32), preferred_element_type=jnp.float32)
        return gradient + residual[index].astype(jnp.float32)

    def add_left(total, index):
        merged = merge_one(index)
        return (total + jnp.dot(merged, q_start, precision=highest), None)
    order = jnp.arange(replicas, dtype=jnp.int32)
    p_sum, unused = lax.scan(add_left, jnp.zeros((width, q_start.shape[1]), jnp.float32), order)
    gram = jnp.dot(p_sum.T, p_sum, precision=highest)
    lower = jnp.linalg.cholesky(gram)
    p_hat = lax.linalg.triangular_solve(lower, p_sum, left_side=False, lower=True, transpose_a=True)

    def add_right(total, index):
        merged = merge_one(index)
        return (total + jnp.dot(merged.T, p_hat, precision=highest), None)
    q_sum, unused = lax.scan(add_right, jnp.zeros(q_start.shape, jnp.float32), order)
    q_factor = q_sum / replicas

    def new_residual(index):
        merged = merge_one(index)
        return (merged - jnp.dot(p_hat, q_factor.T, precision=highest)).astype(jnp.bfloat16)
    residual_out = lax.map(new_residual, order)
    p_factor = p_hat * jnp.sqrt(jnp.float32(width))
    return (p_factor, q_factor, residual_out)
```

```python
import jax
import jax.numpy as jnp
from jax import lax
from jax.experimental import pallas as pl
from jax.experimental.pallas import tpu as pltpu
from jax.sharding import Mesh
from jax.sharding import PartitionSpec as P

F32 = jnp.float32
BF16 = jnp.bfloat16
NN = (((1,), (0,)), ((), ()))
NT = (((1,), (1,)), ((), ()))
VMEM = pl.BlockSpec(memory_space=pltpu.VMEM)
SMEM = pl.BlockSpec(memory_space=pltpu.SMEM)
XZ = ("x", "z")
COLUMN_BLOCK = 640


def call(kernel, outs, flops, moved):
    several = isinstance(outs, list)
    shapes = [jax.ShapeDtypeStruct(*o) for o in (outs if several else [outs])]

    def run(*operands, scratch=(), smem=()):
        return pl.pallas_call(
            kernel,
            out_shape=shapes if several else shapes[0],
            in_specs=[SMEM if i in smem else VMEM for i in range(len(operands))],
            out_specs=[VMEM] * len(shapes) if several else VMEM,
            scratch_shapes=list(scratch),
            compiler_params=pltpu.CompilerParams(vmem_limit_bytes=40 * 1024 * 1024),
            cost_estimate=pl.CostEstimate(flops=flops, bytes_accessed=moved, transcendentals=0),
        )(*operands)

    return run


def pieces(x):
    high = x.astype(BF16)
    rest = x - high.astype(F32)
    middle = rest.astype(BF16)
    low = (rest - middle.astype(F32)).astype(BF16)
    return high, middle, low


def stacked(x):
    return jnp.concatenate(pieces(x), axis=0)


def folded(y):
    n = y.shape[0] // 3
    return y[:n] + (y[n : 2 * n] + y[2 * n :])


def dot(a, b, dims):
    return lax.dot_general(a, b, dims, preferred_element_type=F32)


def token_terms(q_ref, grads_ref, out_ref):
    q3 = stacked(q_ref[...])
    parts, _, tokens = out_ref.shape
    for j in range(parts):
        out_ref[j] = folded(dot(q3, grads_ref[pl.ds(j * tokens, tokens), :], NT))


def residual_left(q_ref, residual_ref, out_ref):
    q3 = stacked(q_ref[...])
    for b in range(0, out_ref.shape[1], COLUMN_BLOCK):
        block = pl.ds(b, COLUMN_BLOCK)
        out_ref[:, block] = folded(dot(q3, residual_ref[block, :], NT))


def left_terms(tokens_ref, acts_ref, base_ref, out_ref):
    z = tokens_ref[0]
    for j in range(1, tokens_ref.shape[0]):
        z = z + tokens_ref[j]
    z3 = stacked(z)
    half = out_ref.shape[1]
    for b in range(0, out_ref.shape[2], COLUMN_BLOCK):
        block = pl.ds(b, COLUMN_BLOCK)
        left = folded(dot(z3, acts_ref[:, block], NN)) + base_ref[:, block]
        out_ref[0, :, block] = left[:half]
        out_ref[1, :, block] = left[half:]


def cut_left(halves_ref, out_ref):
    chunks, rows, width = out_ref.shape
    groups = halves_ref.shape[1] // rows
    per = chunks // groups
    for g in range(groups):
        for i in range(0, per, 2):
            both = pl.ds(i * width, 2 * width)
            here = pl.ds(g * rows, rows)
            total = halves_ref[0, here, both] + halves_ref[1, here, both]
            out_ref[g * per + i] = total[:, :width]
            out_ref[g * per + i + 1] = total[:, width:]


def sum_and_fan(in_ref, out_ref):
    total = in_ref[0]
    for j in range(1, in_ref.shape[0]):
        total = total + in_ref[j]
    for j in range(out_ref.shape[0]):
        out_ref[j] = total


def inverse_factor(gram, n):
    row_at = lax.broadcasted_iota(jnp.int32, (n, 2 * n), 0)
    col_at = lax.broadcasted_iota(jnp.int32, (n, 2 * n), 1)
    unit = (col_at == row_at + n).astype(F32)
    work = jnp.concatenate([gram, unit[:, n:]], axis=1)
    scale = jnp.zeros((n, 1), F32)
    rows_only = row_at[:, :1]
    for k in range(n):
        pivot = work[k : k + 1, k : k + 1]
        scale = jnp.where(rows_only == k, pivot, scale)
        if k < n - 1:
            factor = work[:, k : k + 1] / pivot
            factor = jnp.where(rows_only > k, factor, 0.0)
            work = work - factor * work[k : k + 1, :]
    return work[:, n:] / jnp.sqrt(scale)


def orthonormal(core_ref, own_ref, other_ref, acts_ref, basis_ref, basis3_ref, tokens_ref, left, left3):
    n, width = left.shape
    rows = own_ref.shape[1]
    step = own_ref.shape[2]
    groups = n // (2 * rows)
    per = width // step
    first = core_ref[0] == 0
    for g in range(groups):
        for i in range(0, per, 2):
            at = g * per + i
            mine = jnp.concatenate([own_ref[at], own_ref[at + 1]], axis=1)
            theirs = jnp.concatenate([other_ref[at], other_ref[at + 1]], axis=1)
            both = pl.ds(i * step, 2 * step)
            left[pl.ds(g * rows, rows), both] = jnp.where(first, mine, theirs)
            left[pl.ds(n // 2 + g * rows, rows), both] = jnp.where(first, theirs, mine)
    nine = jnp.zeros((3 * n, 3 * n), F32)
    for b in range(0, width, COLUMN_BLOCK):
        block = pl.ds(b, COLUMN_BLOCK)
        l3 = stacked(left[:, block])
        left3[:, block] = l3
        nine = nine + dot(l3, l3, NT)
    part = lambda i, j: nine[i * n : (i + 1) * n, j * n : (j + 1) * n]
    gram = part(0, 0) + (
        (part(0, 1) + part(1, 0)) + ((part(0, 2) + part(2, 0) + part(1, 1)) + ((part(1, 2) + part(2, 1)) + part(2, 2)))
    )
    high, middle, low = pieces(inverse_factor(gram, n))
    wide = jnp.concatenate([high, high, high, middle, middle, low], axis=1)
    terms = jnp.zeros((3 * n, acts_ref.shape[0]), F32)
    for b in range(0, width, COLUMN_BLOCK):
        block = pl.ds(b, COLUMN_BLOCK)
        l3 = left3[:, block]
        tall = jnp.concatenate([l3, l3[: 2 * n], l3[:n]], axis=0)
        basis = dot(wide, tall, NN)
        basis_ref[:, block] = basis
        b3 = stacked(basis)
        basis3_ref[:, block] = b3
        terms = terms + dot(b3, acts_ref[:, block], NT)
    terms = folded(terms)
    for j in range(tokens_ref.shape[0]):
        tokens_ref[j] = terms


def residual_right(basis3_ref, residual_ref, out_ref, tall_ref):
    n = out_ref.shape[0]
    total = jnp.zeros((3 * n, out_ref.shape[1]), F32)
    for b in range(0, basis3_ref.shape[1], COLUMN_BLOCK):
        block = pl.ds(b, COLUMN_BLOCK)
        b3 = basis3_ref[:, block]
        total = total + dot(b3, residual_ref[block, :], NN)
        six = jnp.concatenate([b3, b3[: 2 * n], b3[:n]], axis=0)
        tall_ref[block, :] = six.T
    out_ref[...] = folded(total)


def right_terms(tokens_ref, base_ref, grads_ref, out_ref):
    total = base_ref[...]
    tokens = tokens_ref.shape[2]
    for j in range(tokens_ref.shape[0]):
        total = total + folded(dot(stacked(tokens_ref[j]), grads_ref[pl.ds(j * tokens, tokens), :], NN))
    half = out_ref.shape[1]
    out_ref[0] = total[:half]
    out_ref[1] = total[half:]


def sum_right(in_ref, out_ref):
    total = in_ref[0]
    for j in range(1, in_ref.shape[0]):
        total = total + in_ref[j]
    out_ref[...] = total


def finish(core_ref, scale_ref, own_ref, other_ref, merged_ref, tall_ref, right_ref, residual_ref):
    first = core_ref[0] == 0
    own, other = own_ref[...], other_ref[...]
    right = jnp.concatenate([jnp.where(first, own, other), jnp.where(first, other, own)], axis=0)
    right = right * scale_ref[0]
    right_ref[...] = right
    high, middle, low = pieces(right)
    six = jnp.concatenate([high, high, high, middle, middle, low], axis=0)
    for b in range(0, merged_ref.shape[0], COLUMN_BLOCK):
        block = pl.ds(b, COLUMN_BLOCK)
        residual_ref[block, :] = (merged_ref[block, :] - dot(tall_ref[block, :], six, NN)).astype(BF16)


def shards(activations, out_grads, residual, q_start):
    acts, grads, resid = activations[0], out_grads[0], residual[0]
    own_tokens, width = acts.shape
    all_tokens, columns = grads.shape
    rank = q_start.shape[1]
    nt, nxz = lax.axis_size("tensor"), lax.axis_size(XZ)
    replicas = lax.axis_size(("x", "z", "core"))
    half = rank // 2
    chunk = half * width // (8 * nxz)
    core = lax.axis_index("core").astype(jnp.int32).reshape(1)
    swap = [(0, 1), (1, 0)]
    qt = q_start.T

    with jax.named_scope("gather_activations"):
        gathered = lax.all_gather(acts, "tensor", axis=0, tiled=True)

    with jax.named_scope("token_terms"):
        z = call(token_terms, ((nt, rank, own_tokens), F32), 2 * 3 * rank * columns * all_tokens, 2**19)(qt, grads)
        z = lax.all_to_all(z, "tensor", 0, 0)
    with jax.named_scope("residual_left"):
        base = call(residual_left, ((rank, width), F32), 2 * 3 * rank * columns * width, 2**21)(qt, resid)
    with jax.named_scope("left_terms"):
        left = call(left_terms, ((2, half, width), F32), 2 * 3 * rank * own_tokens * width, 2**22)(z, acts, base)
    with jax.named_scope("left_sum"):
        left = lax.all_to_all(left, "core", 0, 0)
        left = call(cut_left, ((nxz, 8, chunk), F32), 2**18, 2**20)(left)
        left = lax.all_to_all(left, XZ, 0, 0)
        left = call(sum_and_fan, ((nt, 8, chunk), F32), 2**18, 2**19)(left)
        left = lax.all_to_all(left, "tensor", 0, 0)
        left = call(sum_and_fan, ((nxz, 8, chunk), F32), 2**18, 2**19)(left)
        own = lax.all_to_all(left, XZ, 0, 0)
        other = lax.ppermute(own, "core", swap)
    with jax.named_scope("orthonormal"):
        basis, basis3, tokens = call(
            orthonormal,
            [((rank, width), F32), ((3 * rank, width), BF16), ((nt, rank, own_tokens), F32)],
            2 * 9 * rank * rank * width,
            2**22,
        )(
            core,
            own,
            other,
            acts,
            scratch=(pltpu.VMEM((rank, width), F32), pltpu.VMEM((3 * rank, width), BF16)),
            smem=(0,),
        )
        tokens = lax.all_to_all(tokens, "tensor", 0, 0)
    with jax.named_scope("residual_right"):
        base, tall = call(
            residual_right, [((rank, columns), F32), ((width, 6 * rank), BF16)], 2 * 3 * rank * columns * width, 2**22
        )(basis3, resid)
    with jax.named_scope("right_terms"):
        right = call(right_terms, ((2, half, columns), F32), 2 * 3 * rank * all_tokens * columns, 2**19)(
            tokens, base, grads
        )
    with jax.named_scope("right_sum"):
        right = lax.all_to_all(right, "core", 0, 0)
        fan = call(sum_and_fan, ((nxz, half, columns), F32), 2**16, 2**18)(right)
        right = lax.all_to_all(fan, XZ, 0, 0)
        own = call(sum_right, ((half, columns), F32), 2**16, 2**18)(right)
        other = lax.ppermute(own, "core", swap)
    with jax.named_scope("merged"):
        gathered, _ = lax.optimization_barrier((gathered, fan))
        merged = lax.dot_general(
            gathered, grads, (((0,), (0,)), ((), ())), preferred_element_type=F32
        ) + resid.astype(F32)
    with jax.named_scope("finish"):
        right, residual_out = call(
            finish, [((rank, columns), F32), ((width, columns), BF16)], 2 * 6 * rank * width * columns, 2**22
        )(core, jnp.full((1,), 1.0 / replicas, F32), own, other, merged, tall, smem=(0, 1))
    with jax.named_scope("p_factor"):
        own_rows = width // nt
        p_factor = lax.dynamic_slice_in_dim(basis, lax.axis_index("tensor") * own_rows, own_rows, 1).T
        p_factor = p_factor * jnp.sqrt(jnp.float32(width))
    return (p_factor, right.T, residual_out[None])


def solution(mesh):
    replicas, tensor = mesh.devices.shape
    zs = 8
    fine = Mesh(mesh.devices.reshape(replicas // (2 * zs), zs, 2, tensor), ("x", "z", "core", "tensor"))
    dp = ("x", "z", "core")
    return jax.shard_map(
        shards,
        mesh=fine,
        in_specs=(
            P(dp, "tensor", None),
            P(dp, None, "tensor"),
            P(dp, None, "tensor"),
            P("tensor", None),
        ),
        out_specs=(P("tensor", None), P("tensor", None), P(dp, None, "tensor")),
        check_vma=False,
    )
```

```python
import jax
import jax.numpy as jnp
from jax import lax
from jax.experimental import pallas as pl
from jax.experimental.pallas import tpu as pltpu
from jax.sharding import Mesh
from jax.sharding import PartitionSpec as P

F32 = jnp.float32
BF16 = jnp.bfloat16
NN = (((1,), (0,)), ((), ()))
NT = (((1,), (1,)), ((), ()))
VMEM = pl.BlockSpec(memory_space=pltpu.VMEM)
SMEM = pl.BlockSpec(memory_space=pltpu.SMEM)
XZ = ("x", "z")
COLUMN_BLOCK = 640
ROW_BLOCK = 2560


def call(kernel, outs, flops, moved):
    several = isinstance(outs, list)
    shapes = [jax.ShapeDtypeStruct(*o) for o in (outs if several else [outs])]

    def run(*operands, scratch=(), smem=()):
        return pl.pallas_call(
            kernel,
            out_shape=shapes if several else shapes[0],
            in_specs=[SMEM if i in smem else VMEM for i in range(len(operands))],
            out_specs=[VMEM] * len(shapes) if several else VMEM,
            scratch_shapes=list(scratch),
            compiler_params=pltpu.CompilerParams(vmem_limit_bytes=16 * 1024 * 1024),
            cost_estimate=pl.CostEstimate(flops=flops, bytes_accessed=moved, transcendentals=0),
        )(*operands)

    return run


def pieces(x):
    high = x.astype(BF16)
    rest = x - high.astype(F32)
    middle = rest.astype(BF16)
    low = (rest - middle.astype(F32)).astype(BF16)
    return high, middle, low


def stacked(x):
    return jnp.concatenate(pieces(x), axis=0)


def folded(y):
    n = y.shape[0] // 3
    return y[:n] + (y[n : 2 * n] + y[2 * n :])


def six_left(x):
    high, middle, low = pieces(x)
    return jnp.concatenate([high, high, high, middle, middle, low], axis=1)


def six_right(x):
    high, middle, low = pieces(x)
    return jnp.concatenate([high, middle, low, high, middle, high], axis=0)


def dot(a, b, dims):
    return lax.dot_general(a, b, dims, preferred_element_type=F32)


def token_terms(q_ref, grads_ref, out_ref):
    q3 = stacked(q_ref[...])
    parts, _, tokens = out_ref.shape
    for j in range(parts):
        out_ref[j] = folded(dot(q3, grads_ref[pl.ds(j * tokens, tokens), :], NT))


def residual_left(q_ref, residual_ref, out_ref):
    q3 = stacked(q_ref[...])
    for b in range(0, out_ref.shape[1], COLUMN_BLOCK):
        block = pl.ds(b, COLUMN_BLOCK)
        out_ref[:, block] = folded(dot(q3, residual_ref[block, :], NT))


def left_terms(tokens_ref, acts_ref, base_ref, out_ref):
    z = tokens_ref[0]
    for j in range(1, tokens_ref.shape[0]):
        z = z + tokens_ref[j]
    z3 = stacked(z)
    half = out_ref.shape[1]
    for b in range(0, out_ref.shape[2], COLUMN_BLOCK):
        block = pl.ds(b, COLUMN_BLOCK)
        left = folded(dot(z3, acts_ref[:, block], NN)) + base_ref[:, block]
        out_ref[0, :, block] = left[:half]
        out_ref[1, :, block] = left[half:]


def cut_left(halves_ref, out_ref):
    chunks, rows, width = out_ref.shape
    groups = halves_ref.shape[1] // rows
    per = chunks // groups
    for i in range(per):
        block = pl.ds(i * width, width)
        total = halves_ref[0, :, block] + halves_ref[1, :, block]
        for g in range(groups):
            out_ref[g * per + i] = total[g * rows : (g + 1) * rows]


def sum_and_fan(in_ref, out_ref):
    total = in_ref[0]
    for j in range(1, in_ref.shape[0]):
        total = total + in_ref[j]
    for j in range(out_ref.shape[0]):
        out_ref[j] = total


def inverse_factor(gram, n):
    row_at = lax.broadcasted_iota(jnp.int32, (n, 2 * n), 0)
    col_at = lax.broadcasted_iota(jnp.int32, (n, 2 * n), 1)
    unit = (col_at == row_at + n).astype(F32)
    work = jnp.concatenate([gram, unit[:, n:]], axis=1)
    scale = jnp.zeros((n, 1), F32)
    rows_only = row_at[:, :1]
    for k in range(n):
        pivot = work[k : k + 1, k : k + 1]
        scale = jnp.where(rows_only == k, pivot, scale)
        if k < n - 1:
            factor = work[:, k : k + 1] / pivot
            factor = jnp.where(rows_only > k, factor, 0.0)
            work = work - factor * work[k : k + 1, :]
    return work[:, n:] / jnp.sqrt(scale)


def joined(ref, groups, i):
    per = ref.shape[0] // groups
    return jnp.concatenate([ref[g * per + i] for g in range(groups)], axis=0)


def token_products(left_ref, own_ref, sibling_ref, tokens_ref):
    chunks, rows, width = left_ref.shape
    half = tokens_ref.shape[1] // 2
    groups = half // rows
    own = jnp.zeros((3 * half, own_ref.shape[0]), F32)
    sibling = own
    for i in range(chunks // groups):
        block = pl.ds(i * width, width)
        l3 = stacked(joined(left_ref, groups, i))
        own = own + dot(l3, own_ref[:, block], NT)
        sibling = sibling + dot(l3, sibling_ref[:, block], NT)
    both = jnp.concatenate([folded(own), folded(sibling)], axis=0)
    for j in range(tokens_ref.shape[0]):
        tokens_ref[j] = both


def residual_right(left_ref, own_ref, sibling_ref, out_ref):
    chunks, rows, width = left_ref.shape
    half = out_ref.shape[0]
    groups = half // rows
    total = jnp.zeros((3 * half, out_ref.shape[1]), F32)
    for i in range(chunks // groups):
        block = pl.ds(i * width, width)
        l3 = stacked(joined(left_ref, groups, i))
        total = total + dot(l3, own_ref[block, :], NN) + dot(l3, sibling_ref[block, :], NN)
    out_ref[...] = folded(total)


def orthonormal(core_ref, at_ref, own_ref, other_ref, basis3_ref, factor_ref, inverse_ref, left3, basis):
    n, width = basis.shape
    step = own_ref.shape[2]
    groups = n // (2 * own_ref.shape[1])
    first = core_ref[0] == 0
    nine = jnp.zeros((3 * n, 3 * n), F32)
    for i in range(width // step):
        block = pl.ds(i * step, step)
        mine, theirs = joined(own_ref, groups, i), joined(other_ref, groups, i)
        l3 = stacked(jnp.concatenate([jnp.where(first, mine, theirs), jnp.where(first, theirs, mine)], axis=0))
        left3[:, block] = l3
        nine = nine + dot(l3, l3, NT)
    part = lambda i, j: nine[i * n : (i + 1) * n, j * n : (j + 1) * n]
    gram = part(0, 0) + (
        (part(0, 1) + part(1, 0)) + ((part(0, 2) + part(2, 0) + part(1, 1)) + ((part(1, 2) + part(2, 1)) + part(2, 2)))
    )
    inverse = inverse_factor(gram, n)
    inverse_ref[...] = inverse
    wide = six_left(inverse)
    for b in range(0, width, COLUMN_BLOCK):
        block = pl.ds(b, COLUMN_BLOCK)
        l3 = left3[:, block]
        part_of = dot(wide, jnp.concatenate([l3, l3[: 2 * n], l3[:n]], axis=0), NN)
        basis[:, block] = part_of
        basis3_ref[:, block] = stacked(part_of)
    columns = factor_ref.shape[1]
    own = pl.ds(pl.multiple_of(at_ref[0] * columns, 128), columns)
    factor_ref[...] = basis[:, own] * jnp.sqrt(F32(width))


def right_terms(tokens_ref, base_ref, own_ref, sibling_ref, out_ref):
    total = base_ref[...]
    half = total.shape[0]
    blocks, _, tokens = tokens_ref.shape
    for j in range(blocks):
        here = pl.ds(j * tokens, tokens)
        total = total + folded(
            dot(stacked(tokens_ref[j, :half]), own_ref[here, :], NN)
            + dot(stacked(tokens_ref[j, half:]), sibling_ref[here, :], NN)
        )
    for j in range(out_ref.shape[0]):
        out_ref[j] = total


def sum_right(in_ref, out_ref):
    total = in_ref[0]
    for j in range(1, in_ref.shape[0]):
        total = total + in_ref[j]
    out_ref[...] = total


def right_and_base(core_ref, scale_ref, own_ref, other_ref, inverse_ref, basis3_ref, residual_ref, right_ref, out_ref):
    first = core_ref[0] == 0
    own, other = own_ref[...], other_ref[...]
    raw = jnp.concatenate([jnp.where(first, own, other), jnp.where(first, other, own)], axis=0)
    right = dot(six_left(inverse_ref[...]), six_right(raw), NN) * scale_ref[0]
    right_ref[...] = right
    high, middle, low = pieces(right)
    right_t = jnp.concatenate([high, high, high, middle, middle, low], axis=0).T
    n = right.shape[0]
    for b in range(0, out_ref.shape[0], COLUMN_BLOCK):
        block = pl.ds(b, COLUMN_BLOCK)
        b3 = basis3_ref[:, block]
        product = dot(right_t, jnp.concatenate([b3, b3[: 2 * n], b3[:n]], axis=0), NN)
        out_ref[block, :] = residual_ref[block, :].astype(F32) - product.T


def residual_terms(grads_ref, acts_ref, base_ref, out_ref, grads_t):
    @pl.when(pl.program_id(0) == 0)
    def _():
        grads_t[...] = grads_ref[...].T

    gradient_t = dot(grads_t[...], acts_ref[...], NN)
    out_ref[...] = (gradient_t.T + base_ref[...]).astype(BF16)


def shards(activations, out_grads, residual, q_start):
    acts, grads, resid = activations[0], out_grads[0], residual[0]
    own_tokens, width = acts.shape
    all_tokens, columns = grads.shape
    rank = q_start.shape[1]
    nt, nxz = lax.axis_size("tensor"), lax.axis_size(XZ)
    replicas = lax.axis_size(("x", "z", "core"))
    half = rank // 2
    chunk = (nxz, 4, half * width // (4 * nxz))
    core = lax.axis_index("core").astype(jnp.int32).reshape(1)
    swap = [(0, 1), (1, 0)]
    qt = q_start.T

    with jax.named_scope("gather_activations"):
        gathered = lax.all_gather(acts, "tensor", axis=0, tiled=True)

    with jax.named_scope("token_terms"):
        z = call(token_terms, ((nt, rank, own_tokens), F32), 2 * 3 * rank * columns * all_tokens, 2**19)(qt, grads)
        z = lax.all_to_all(z, "tensor", 0, 0)
    with jax.named_scope("residual_left"):
        base = call(residual_left, ((rank, width), F32), 2 * 3 * rank * columns * width, 2**22)(qt, resid)
    with jax.named_scope("sibling"):
        base, *mine = lax.optimization_barrier((base, resid, acts, grads))
        resid_sib, acts_sib, grads_sib = [lax.ppermute(x, "core", swap) for x in mine]
    with jax.named_scope("left_terms"):
        left = call(left_terms, ((2, half, width), F32), 2 * 3 * rank * own_tokens * width, 2**22)(z, acts, base)
    with jax.named_scope("left_sum"):
        left = lax.all_to_all(left, "core", 0, 0)
        left = call(cut_left, (chunk, F32), 2**18, 2**20)(left)
        left = lax.all_to_all(left, XZ, 0, 0)
        left = call(sum_and_fan, ((nt,) + chunk[1:], F32), 2**18, 2**19)(left)
        left = lax.all_to_all(left, "tensor", 0, 0)
        left = call(sum_and_fan, (chunk, F32), 2**18, 2**19)(left)
        left_own = lax.all_to_all(left, XZ, 0, 0)
    with jax.named_scope("token_products"):
        tokens = call(
            token_products, ((nt, rank, own_tokens), F32), 2 * 3 * rank * own_tokens * width, 2**22
        )(left_own, acts, acts_sib)
        tokens = lax.all_to_all(tokens, "tensor", 0, 0)
    with jax.named_scope("residual_right"):
        base = call(residual_right, ((half, columns), F32), 2 * 3 * rank * columns * width, 2**22)(
            left_own, resid, resid_sib
        )
    with jax.named_scope("orthonormal"):
        left_other = lax.ppermute(left_own, "core", swap)
    with jax.named_scope("right_terms"):
        right = call(right_terms, ((nxz, half, columns), F32), 2 * 3 * rank * all_tokens * columns, 2**19)(
            tokens, base, grads, grads_sib
        )
    with jax.named_scope("right_sum"):
        right = lax.all_to_all(right, XZ, 0, 0)
    with jax.named_scope("orthonormal"):
        at = lax.axis_index("tensor").astype(jnp.int32).reshape(1)
        basis3, p_factor, inverse = call(
            orthonormal,
            [((3 * rank, width), BF16), ((rank, width // nt), F32), ((rank, rank), F32)],
            2**32,
            2**22,
        )(
            core,
            at,
            left_own,
            left_other,
            scratch=(pltpu.VMEM((3 * rank, width), BF16), pltpu.VMEM((rank, width), F32)),
            smem=(0, 1),
        )
    with jax.named_scope("right_sum"):
        right, basis3 = lax.optimization_barrier((right, basis3))
        own = call(sum_right, ((half, columns), F32), 2**16, 2**18)(right)
        other = lax.ppermute(own, "core", swap)
    with jax.named_scope("right_and_base"):
        right, base = call(
            right_and_base, [((rank, columns), F32), ((width, columns), F32)], 2 * 6 * rank * width * columns, 2**22
        )(core, jnp.full((1,), 1.0 / replicas, F32), own, other, inverse, basis3, resid, smem=(0, 1))
    with jax.named_scope("residual_out"):
        residual_out = pl.pallas_call(
            residual_terms,
            grid=(width // ROW_BLOCK,),
            out_shape=jax.ShapeDtypeStruct((width, columns), BF16),
            in_specs=[
                pl.BlockSpec((all_tokens, columns), lambda i: (0, 0)),
                pl.BlockSpec((all_tokens, ROW_BLOCK), lambda i: (0, i)),
                pl.BlockSpec((ROW_BLOCK, columns), lambda i: (i, 0)),
            ],
            out_specs=pl.BlockSpec((ROW_BLOCK, columns), lambda i: (i, 0)),
            scratch_shapes=[pltpu.VMEM((columns, all_tokens), BF16)],
            compiler_params=pltpu.CompilerParams(vmem_limit_bytes=54 * 1024 * 1024),
            cost_estimate=pl.CostEstimate(flops=2**31, bytes_accessed=2**24, transcendentals=0),
        )(grads, gathered, base)
    return (p_factor.T, right.T, residual_out[None])


def solution(mesh):
    replicas, tensor = mesh.devices.shape
    zs = 8
    fine = Mesh(mesh.devices.reshape(replicas // (2 * zs), zs, 2, tensor), ("x", "z", "core", "tensor"))
    dp = ("x", "z", "core")
    return jax.shard_map(
        shards,
        mesh=fine,
        in_specs=(
            P(dp, "tensor", None),
            P(dp, None, "tensor"),
            P(dp, None, "tensor"),
            P("tensor", None),
        ),
        out_specs=(P("tensor", None), P("tensor", None), P(dp, None, "tensor")),
        check_vma=False,
    )
```

```python
import jax
import jax.numpy as jnp
from jax import lax
from jax.experimental import pallas as pl
from jax.experimental.pallas import tpu as pltpu
from jax.sharding import Mesh
from jax.sharding import PartitionSpec as P

F32 = jnp.float32
BF16 = jnp.bfloat16
NN = (((1,), (0,)), ((), ()))
NT = (((1,), (1,)), ((), ()))
VMEM = pl.BlockSpec(memory_space=pltpu.VMEM)
SMEM = pl.BlockSpec(memory_space=pltpu.SMEM)
XZ = ("x", "z")
COLUMN_BLOCK = 1280
ROW_BLOCK = 2560


def call(kernel, outs, flops, moved):
    several = isinstance(outs, list)
    shapes = [jax.ShapeDtypeStruct(*o) for o in (outs if several else [outs])]

    def run(*operands, scratch=(), smem=()):
        return pl.pallas_call(
            kernel,
            out_shape=shapes if several else shapes[0],
            in_specs=[SMEM if i in smem else VMEM for i in range(len(operands))],
            out_specs=[VMEM] * len(shapes) if several else VMEM,
            scratch_shapes=list(scratch),
            compiler_params=pltpu.CompilerParams(vmem_limit_bytes=16 * 1024 * 1024),
            cost_estimate=pl.CostEstimate(flops=flops, bytes_accessed=moved, transcendentals=0),
        )(*operands)

    return run


def pieces(x):
    high = x.astype(BF16)
    rest = x - high.astype(F32)
    middle = rest.astype(BF16)
    low = (rest - middle.astype(F32)).astype(BF16)
    return high, middle, low


def stacked(x):
    return jnp.concatenate(pieces(x), axis=0)


def folded(y):
    n = y.shape[0] // 3
    return y[:n] + (y[n : 2 * n] + y[2 * n :])


def six_left(x):
    high, middle, low = pieces(x)
    return jnp.concatenate([high, high, high, middle, middle, low], axis=1)


def six_right(x):
    high, middle, low = pieces(x)
    return jnp.concatenate([high, middle, low, high, middle, high], axis=0)


def dot(a, b, dims):
    return lax.dot_general(a, b, dims, preferred_element_type=F32)


def token_terms(q_ref, grads_ref, out_ref):
    q3 = stacked(q_ref[...])
    parts, _, tokens = out_ref.shape
    for j in range(parts):
        out_ref[j] = folded(dot(q3, grads_ref[pl.ds(j * tokens, tokens), :], NT))


def residual_left(q_ref, residual_ref, out_ref):
    q3 = stacked(q_ref[...])
    for b in range(0, out_ref.shape[1], COLUMN_BLOCK):
        block = pl.ds(b, COLUMN_BLOCK)
        out_ref[:, block] = folded(dot(q3, residual_ref[block, :], NT))


def left_terms(tokens_ref, acts_ref, base_ref, out_ref):
    z = tokens_ref[0]
    for j in range(1, tokens_ref.shape[0]):
        z = z + tokens_ref[j]
    z3 = stacked(z)
    half = out_ref.shape[1]
    for b in range(0, out_ref.shape[2], COLUMN_BLOCK):
        block = pl.ds(b, COLUMN_BLOCK)
        left = folded(dot(z3, acts_ref[:, block], NN)) + base_ref[:, block]
        out_ref[0, :, block] = left[:half]
        out_ref[1, :, block] = left[half:]


def cut_left(halves_ref, out_ref):
    chunks, rows, width = out_ref.shape
    groups = halves_ref.shape[1] // rows
    per = chunks // groups
    for i in range(per):
        block = pl.ds(i * width, width)
        total = halves_ref[0, :, block] + halves_ref[1, :, block]
        for g in range(groups):
            out_ref[g * per + i] = total[g * rows : (g + 1) * rows]


def sum_and_fan(in_ref, out_ref):
    total = in_ref[0]
    for j in range(1, in_ref.shape[0]):
        total = total + in_ref[j]
    for j in range(out_ref.shape[0]):
        out_ref[j] = total


def inverse_factor(gram, n):
    row_at = lax.broadcasted_iota(jnp.int32, (n, 2 * n), 0)
    col_at = lax.broadcasted_iota(jnp.int32, (n, 2 * n), 1)
    unit = (col_at == row_at + n).astype(F32)
    work = jnp.concatenate([gram, unit[:, n:]], axis=1)
    scale = jnp.zeros((n, 1), F32)
    rows_only = row_at[:, :1]
    for k in range(n):
        pivot = work[k : k + 1, k : k + 1]
        scale = jnp.where(rows_only == k, pivot, scale)
        if k < n - 1:
            factor = work[:, k : k + 1] / pivot
            factor = jnp.where(rows_only > k, factor, 0.0)
            work = work - factor * work[k : k + 1, :]
    return work[:, n:] / jnp.sqrt(scale)


def joined(ref, groups, i):
    per = ref.shape[0] // groups
    return jnp.concatenate([ref[g * per + i] for g in range(groups)], axis=0)


def token_products(left_ref, own_ref, sibling_ref, tokens_ref):
    chunks, rows, width = left_ref.shape
    half = tokens_ref.shape[1] // 2
    groups = half // rows
    own = jnp.zeros((3 * half, own_ref.shape[0]), F32)
    sibling = own
    for i in range(chunks // groups):
        block = pl.ds(i * width, width)
        l3 = stacked(joined(left_ref, groups, i))
        own = own + dot(l3, own_ref[:, block], NT)
        sibling = sibling + dot(l3, sibling_ref[:, block], NT)
    both = jnp.concatenate([folded(own), folded(sibling)], axis=0)
    for j in range(tokens_ref.shape[0]):
        tokens_ref[j] = both


def residual_right(left_ref, own_ref, sibling_ref, out_ref):
    chunks, rows, width = left_ref.shape
    half = out_ref.shape[0]
    groups = half // rows
    total = jnp.zeros((3 * half, out_ref.shape[1]), F32)
    for i in range(chunks // groups):
        block = pl.ds(i * width, width)
        l3 = stacked(joined(left_ref, groups, i))
        total = total + dot(l3, own_ref[block, :], NN) + dot(l3, sibling_ref[block, :], NN)
    out_ref[...] = folded(total)


def orthonormal(core_ref, at_ref, own_ref, other_ref, basis3_ref, factor_ref, inverse_ref, left3, basis):
    n, width = basis.shape
    step = own_ref.shape[2]
    groups = n // (2 * own_ref.shape[1])
    first = core_ref[0] == 0
    nine = jnp.zeros((3 * n, 3 * n), F32)
    for i in range(width // step):
        block = pl.ds(i * step, step)
        mine, theirs = joined(own_ref, groups, i), joined(other_ref, groups, i)
        l3 = stacked(jnp.concatenate([jnp.where(first, mine, theirs), jnp.where(first, theirs, mine)], axis=0))
        left3[:, block] = l3
        nine = nine + dot(l3, l3, NT)
    part = lambda i, j: nine[i * n : (i + 1) * n, j * n : (j + 1) * n]
    gram = part(0, 0) + (
        (part(0, 1) + part(1, 0)) + ((part(0, 2) + part(2, 0) + part(1, 1)) + ((part(1, 2) + part(2, 1)) + part(2, 2)))
    )
    inverse = inverse_factor(gram, n)
    inverse_ref[...] = inverse
    wide = six_left(inverse)
    for b in range(0, width, COLUMN_BLOCK):
        block = pl.ds(b, COLUMN_BLOCK)
        l3 = left3[:, block]
        part_of = dot(wide, jnp.concatenate([l3, l3[: 2 * n], l3[:n]], axis=0), NN)
        basis[:, block] = part_of
        basis3_ref[:, block] = stacked(part_of)
    columns = factor_ref.shape[1]
    own = pl.ds(pl.multiple_of(at_ref[0] * columns, 128), columns)
    factor_ref[...] = basis[:, own] * jnp.sqrt(F32(width))


def right_terms(tokens_ref, base_ref, own_ref, sibling_ref, out_ref):
    total = base_ref[...]
    half = total.shape[0]
    blocks, _, tokens = tokens_ref.shape
    for j in range(blocks):
        here = pl.ds(j * tokens, tokens)
        total = total + folded(
            dot(stacked(tokens_ref[j, :half]), own_ref[here, :], NN)
            + dot(stacked(tokens_ref[j, half:]), sibling_ref[here, :], NN)
        )
    for j in range(out_ref.shape[0]):
        out_ref[j] = total


def sum_right(in_ref, out_ref):
    total = in_ref[0]
    for j in range(1, in_ref.shape[0]):
        total = total + in_ref[j]
    out_ref[...] = total


def right_and_base(
    core_ref, scale_ref, own_ref, other_ref, inverse_ref, basis3_ref, residual_ref, grads_ref,
    right_ref, out_ref, grads_t_ref,
):
    grads_t_ref[...] = grads_ref[...].T
    first = core_ref[0] == 0
    own, other = own_ref[...], other_ref[...]
    raw = jnp.concatenate([jnp.where(first, own, other), jnp.where(first, other, own)], axis=0)
    right = dot(six_left(inverse_ref[...]), six_right(raw), NN) * scale_ref[0]
    right_ref[...] = right
    high, middle, low = pieces(right)
    right_t = jnp.concatenate([high, high, high, middle, middle, low], axis=0).T
    n = right.shape[0]
    for b in range(0, out_ref.shape[0], COLUMN_BLOCK):
        block = pl.ds(b, COLUMN_BLOCK)
        b3 = basis3_ref[:, block]
        product = dot(right_t, jnp.concatenate([b3, b3[: 2 * n], b3[:n]], axis=0), NN)
        out_ref[block, :] = residual_ref[block, :].astype(F32) - product.T


def residual_terms(grads_t_ref, acts_ref, base_ref, out_ref):
    gradient_t = dot(grads_t_ref[...], acts_ref[...], NN)
    out_ref[...] = (gradient_t.T + base_ref[...]).astype(BF16)


def shards(activations, out_grads, residual, q_start):
    acts, grads, resid = activations[0], out_grads[0], residual[0]
    own_tokens, width = acts.shape
    all_tokens, columns = grads.shape
    rank = q_start.shape[1]
    nt, nxz = lax.axis_size("tensor"), lax.axis_size(XZ)
    replicas = lax.axis_size(("x", "z", "core"))
    half = rank // 2
    chunk = (nxz, 4, half * width // (4 * nxz))
    core = lax.axis_index("core").astype(jnp.int32).reshape(1)
    swap = [(0, 1), (1, 0)]
    qt = q_start.T

    with jax.named_scope("gather_activations"):
        gathered = lax.all_gather(acts, "tensor", axis=0, tiled=True)

    with jax.named_scope("token_terms"):
        z = call(token_terms, ((nt, rank, own_tokens), F32), 2 * 3 * rank * columns * all_tokens, 2**19)(qt, grads)
        z = lax.all_to_all(z, "tensor", 0, 0)
    with jax.named_scope("residual_left"):
        base = call(residual_left, ((rank, width), F32), 2 * 3 * rank * columns * width, 2**22)(qt, resid)
    with jax.named_scope("sibling"):
        base, *mine = lax.optimization_barrier((base, resid, acts, grads))
        resid_sib, acts_sib, grads_sib = [lax.ppermute(x, "core", swap) for x in mine]
    with jax.named_scope("left_terms"):
        left = call(left_terms, ((2, half, width), F32), 2 * 3 * rank * own_tokens * width, 2**22)(z, acts, base)
    with jax.named_scope("left_sum"):
        left = lax.all_to_all(left, "core", 0, 0)
        left = call(cut_left, (chunk, F32), 2**18, 2**20)(left)
        left = lax.all_to_all(left, XZ, 0, 0)
        left = call(sum_and_fan, ((nt,) + chunk[1:], F32), 2**18, 2**19)(left)
        left = lax.all_to_all(left, "tensor", 0, 0)
        left = call(sum_and_fan, (chunk, F32), 2**18, 2**19)(left)
        left_own = lax.all_to_all(left, XZ, 0, 0)
    with jax.named_scope("token_products"):
        tokens = call(
            token_products, ((nt, rank, own_tokens), F32), 2 * 3 * rank * own_tokens * width, 2**22
        )(left_own, acts, acts_sib)
        tokens = lax.all_to_all(tokens, "tensor", 0, 0)
    with jax.named_scope("residual_right"):
        base = call(residual_right, ((half, columns), F32), 2 * 3 * rank * columns * width, 2**22)(
            left_own, resid, resid_sib
        )
    with jax.named_scope("orthonormal"):
        left_other = lax.ppermute(left_own, "core", swap)
    with jax.named_scope("right_terms"):
        right = call(right_terms, ((nxz, half, columns), F32), 2 * 3 * rank * all_tokens * columns, 2**19)(
            tokens, base, grads, grads_sib
        )
    with jax.named_scope("right_sum"):
        right = lax.all_to_all(right, XZ, 0, 0)
    with jax.named_scope("orthonormal"):
        at = lax.axis_index("tensor").astype(jnp.int32).reshape(1)
        basis3, p_factor, inverse = call(
            orthonormal,
            [((3 * rank, width), BF16), ((rank, width // nt), F32), ((rank, rank), F32)],
            2**32,
            2**22,
        )(
            core,
            at,
            left_own,
            left_other,
            scratch=(pltpu.VMEM((3 * rank, width), BF16), pltpu.VMEM((rank, width), F32)),
            smem=(0, 1),
        )
    with jax.named_scope("right_sum"):
        right, basis3 = lax.optimization_barrier((right, basis3))
        own = call(sum_right, ((half, columns), F32), 2**16, 2**18)(right)
        other = lax.ppermute(own, "core", swap)
    with jax.named_scope("right_and_base"):
        right, base, grads_t = call(
            right_and_base,
            [((rank, columns), F32), ((width, columns), F32), ((columns, all_tokens), BF16)],
            2 * 6 * rank * width * columns,
            2**22,
        )(core, jnp.full((1,), 1.0 / replicas, F32), own, other, inverse, basis3, resid, grads, smem=(0, 1))
    with jax.named_scope("residual_out"):
        residual_out = pl.pallas_call(
            residual_terms,
            grid=(width // ROW_BLOCK,),
            out_shape=jax.ShapeDtypeStruct((width, columns), BF16),
            in_specs=[
                pl.BlockSpec((columns, all_tokens), lambda i: (0, 0)),
                pl.BlockSpec((all_tokens, ROW_BLOCK), lambda i: (0, i)),
                pl.BlockSpec((ROW_BLOCK, columns), lambda i: (i, 0)),
            ],
            out_specs=pl.BlockSpec((ROW_BLOCK, columns), lambda i: (i, 0)),
            compiler_params=pltpu.CompilerParams(vmem_limit_bytes=54 * 1024 * 1024),
            cost_estimate=pl.CostEstimate(flops=2**31, bytes_accessed=2**24, transcendentals=0),
        )(grads_t, gathered, base)
    return (p_factor.T, right.T, residual_out[None])


def solution(mesh):
    replicas, tensor = mesh.devices.shape
    zs = 8
    fine = Mesh(mesh.devices.reshape(replicas // (2 * zs), zs, 2, tensor), ("x", "z", "core", "tensor"))
    dp = ("x", "z", "core")
    return jax.shard_map(
        shards,
        mesh=fine,
        in_specs=(
            P(dp, "tensor", None),
            P(dp, None, "tensor"),
            P(dp, None, "tensor"),
            P("tensor", None),
        ),
        out_specs=(P("tensor", None), P("tensor", None), P(dp, None, "tensor")),
        check_vma=False,
    )
```
